32 devices in a mesh: gy: 8 (over z, core), gx: 4 (over y, x).
Axes of the slice: x: 2, y: 2, z: 4, core: 2. Of those that a mesh axis runs over, the one named last changes fastest.
Arguments:
- e_field: float32 [3, 4, 512, 512], P(None, None, 'gy', 'gx'), may hold values from -6 to 6
- h_field: float32 [3, 4, 512, 512], P(None, None, 'gy', 'gx'), may hold values from -6 to 6
- j_field: float32 [3, 4, 512, 512], P(None, None, 'gy', 'gx'), may hold values from -3 to 3
- material: int32 [4, 512, 512], P(None, 'gy', 'gx'), may hold values from 0 to 31
- material_table: float32 [4, 32], replicated, may hold values from 0.05 to 1
- dft_e: float32 [3, 2, 3, 4, 512, 512], P(None, None, None, None, 'gy', 'gx'), may hold values from -5 to 7
- dft_h: float32 [3, 2, 3, 4, 512, 512], P(None, None, None, None, 'gy', 'gx'), may hold values from -5 to 7
- skin_cell: int32 [32, 32, 128], P(('gy', 'gx')), may hold values from 0 to 32767, as said below
- counts: int32 [32, 32], P(('gy', 'gx')), may hold values from 0 to 128, as said below
- patch_slot: int32 [32, 32, 128], P(('gy', 'gx')), may hold values from 0 to 65535
- area: float32 [3, 2048, 1024], P(None, 'gy', 'gx'), may hold values from -0.5 to 1.5
Outputs:
- e_next: float32 [3, 4, 512, 512], P(None, None, 'gy', 'gx')
- j_next: float32 [3, 4, 512, 512], P(None, None, 'gy', 'gx')
- dft_e_next: float32 [3, 2, 3, 4, 512, 512], P(None, None, None, None, 'gy', 'gx')
- dft_h_next: float32 [3, 2, 3, 4, 512, 512], P(None, None, None, None, 'gy', 'gx')
- point_density: float32 [3, 2048, 1024], P(None, 'gy', 'gx')
- avg_density: float32 [3, 2048, 1024], P(None, 'gy', 'gx')
The draws below stay inside these ranges and needn't reach their ends.
Inputs may be any that keep to these rules, and one draw needn't show every extreme that they name: Within one source block s the entries skin_cell[s, :, :] are distinct. Some owner block d has counts[s, d] = 128 for every source block s.
All inputs are finite; a program needn't handle non-finite values.
Results may differ from the reference program's by a relative error of at most 0.0003.
Values sent between devices are 32-bit elements; how exact they have to be, the bound alone decides.
A program may use at most 192 MiB of HBM per device.

```python
import math
import jax
import jax.numpy as jnp
from jax import lax

PLANES = 4
RX = 64
CY = 128
FREQS = 3
MAT = 32
STEP = 1000
CAP = 128
PU = 256
PV = 256
HALF = 100
BLOCKS = 32
NX = 512
NY = 512
U = 2048
V = 1024
N_GY = 8
N_GX = 4


def draw_material_table(key, part):
    low_end = jnp.array([0.5, 0.2, 0.5, 0.05], jnp.float32)[:, None]
    high_end = jnp.array([1.0, 0.6, 0.98, 0.5], jnp.float32)[:, None]
    uniform_part = jax.random.uniform(key, (4, MAT), jnp.float32)
    return low_end + (high_end - low_end) * uniform_part


def spectrum_draw(key, component):
    shape = (FREQS, 2, 3, PLANES, NX, NY)
    offset_base = jnp.zeros((2, 3), jnp.float32).at[0, component].set(2.0).reshape(1, 2, 3, 1, 1, 1)
    return jnp.clip(jax.random.normal(key, shape, jnp.float32), -5.0, 5.0) + offset_base


def draw_dft_e(key, part):
    return spectrum_draw(jax.random.fold_in(key, 11), 0)


def draw_dft_h(key, part):
    return spectrum_draw(jax.random.fold_in(key, 23), 1)


def draw_skin_cell(key, part):
    block_keys = jax.random.split(jax.random.fold_in(key, 5), BLOCKS)
    cell_total = PLANES * RX * CY

    def per_block(block_key):
        return jax.random.permutation(block_key, cell_total)[:BLOCKS * CAP]
    return jax.vmap(per_block)(block_keys).reshape(BLOCKS, BLOCKS, CAP).astype(jnp.int32)


def draw_counts(key, part):
    key_level, key_count, key_column = jax.random.split(jax.random.fold_in(key, 7), 3)
    levels = jax.random.randint(key_level, (BLOCKS,), 1, 5)
    top_count = CAP * levels // 4 + 1
    raw_count = jax.random.randint(key_count, (BLOCKS, BLOCKS), 0, jnp.broadcast_to(top_count[None, :], (BLOCKS, BLOCKS)))
    hot_column = jax.random.randint(key_column, (), 0, BLOCKS)
    column_ids = jnp.arange(BLOCKS, dtype=jnp.int32)[None, :]
    return jnp.where(column_ids == hot_column, CAP, raw_count).astype(jnp.int32)


def draw_patch_slot(key, part):
    return jax.random.randint(jax.random.fold_in(key, 13), (BLOCKS, BLOCKS, CAP), 0, PU * PV).astype(jnp.int32)


def plant(entries, key, least, largest):
    longest = entries.shape.index(max(entries.shape))
    spots = []
    for shift in (0, 1):
        where = [jax.random.randint(jax.random.fold_in(key, axis), (), 0, length) for axis, length in enumerate(entries.shape)]
        where[longest] = (where[longest] + shift) % entries.shape[longest]
        spots.append(tuple(where))
    return entries.at[spots[0]].set(least).at[spots[1]].set(largest)


def block_levels(own_key, shape, cuts, smallest, largest):
    def one(dim, shards_of):
        steps = jax.random.uniform(jax.random.fold_in(jax.random.fold_in(own_key, 6), dim), (shards_of,), jnp.float32, smallest / len(cuts), largest / len(cuts))
        return jnp.repeat(jnp.exp(steps), shape[dim] // shards_of).reshape((-1,) + (1,) * (len(shape) - dim - 1))

    loudness = one(*cuts[0])
    for cut in cuts[1:]:
        loudness = loudness * one(*cut)
    return loudness


def gaussian(key, dims, spread, bound, cuts=(), kind=jnp.bfloat16):
    loudness = block_levels(key, dims, cuts, -0.22, 0.18) if cuts else 1.0
    drawn = jax.random.normal(key, dims, jnp.float32) * spread * loudness
    return jnp.minimum(jnp.maximum(drawn, -bound), bound).astype(kind)


def setup_inputs(seed: int = 0) -> dict:
    key_of = jax.random.split(jax.random.key(seed), 12)
    e_field = gaussian(key_of[0], (3, PLANES, NX, NY), 1.0, 6.0, ((2, 8), (3, 4)), jnp.float32)
    h_field = gaussian(key_of[1], (3, PLANES, NX, NY), 1.0, 6.0, ((2, 8), (3, 4)), jnp.float32)
    j_field = gaussian(key_of[2], (3, PLANES, NX, NY), 0.5, 3.0, ((2, 8), (3, 4)), jnp.float32)
    material = plant(jax.random.randint(key_of[3], (PLANES, NX, NY), 0, MAT), jax.random.fold_in(key_of[3], 1), 0, MAT - 1).astype(jnp.int32)
    material_table = draw_material_table(jax.random.fold_in(key_of[11], 71), 0)
    dft_e = draw_dft_e(jax.random.fold_in(key_of[11], 71), 0)
    dft_h = draw_dft_h(jax.random.fold_in(key_of[11], 71), 0)
    skin_cell = draw_skin_cell(jax.random.fold_in(key_of[11], 71), 0)
    counts = draw_counts(jax.random.fold_in(key_of[11], 71), 0)
    patch_slot = draw_patch_slot(jax.random.fold_in(key_of[11], 71), 0)
    area = jnp.clip(-0.5 + 2.0 * jax.random.uniform(key_of[10], (3, U, V), jnp.float32) ** block_levels(key_of[10], (3, U, V), ((1, 8), (2, 4)), -0.2, 0.2), -0.5, 1.5)
    return {"e_field": e_field, "h_field": h_field, "j_field": j_field, "material": material, "material_table": material_table, "dft_e": dft_e, "dft_h": dft_h, "skin_cell": skin_cell, "counts": counts, "patch_slot": patch_slot, "area": area}


FREQ_LIST = (28.0e9, 39.0e9, 60.0e9)
TIME_STEP = 1.9e-13


def phase_list(offset):
    return [2.0 * math.pi * freq_hz * (STEP + offset) * TIME_STEP for freq_hz in FREQ_LIST]


def accumulate(running, field_in, offset):
    pieces = []
    for phase_angle in phase_list(offset):
        pieces.append(jnp.stack([field_in * math.cos(phase_angle), field_in * (-math.sin(phase_angle))]))
    return running + jnp.stack(pieces)


def curl_field(h_field, rows_below, cols_left):
    magnet_x, magnet_y, magnet_z = h_field[0], h_field[1], h_field[2]
    zero_plane = jnp.zeros_like(magnet_x[:1])
    x_below_z = jnp.concatenate([zero_plane, magnet_x[:-1]], 0)
    y_below_z = jnp.concatenate([zero_plane, magnet_y[:-1]], 0)
    y_below_x = jnp.concatenate([rows_below[0][:, None, :], magnet_y[:, :-1, :]], 1)
    z_below_x = jnp.concatenate([rows_below[1][:, None, :], magnet_z[:, :-1, :]], 1)
    x_below_y = jnp.concatenate([cols_left[0][:, :, None], magnet_x[:, :, :-1]], 2)
    z_below_y = jnp.concatenate([cols_left[1][:, :, None], magnet_z[:, :, :-1]], 2)
    curl_x = (magnet_z - z_below_y) - (magnet_y - y_below_z)
    curl_y = (magnet_x - x_below_z) - (magnet_z - z_below_x)
    curl_z = (magnet_y - y_below_x) - (magnet_x - x_below_y)
    return jnp.stack([curl_x, curl_y, curl_z])


def cross_product(left_vec, right_vec):
    return jnp.stack([left_vec[:, 1] * right_vec[:, 2] - left_vec[:, 2] * right_vec[:, 1],
                      left_vec[:, 2] * right_vec[:, 0] - left_vec[:, 0] * right_vec[:, 2],
                      left_vec[:, 0] * right_vec[:, 1] - left_vec[:, 1] * right_vec[:, 0]], 1)


def cross_flux(e_rows, h_rows):
    return 0.5 * (cross_product(e_rows[:, 0], h_rows[:, 0]) + cross_product(e_rows[:, 1], h_rows[:, 1]))


def to_blocks(values):
    leading = values.shape[0]
    grid = values.reshape(leading, PLANES, N_GY, RX, N_GX, CY).transpose(0, 2, 4, 1, 3, 5)
    return grid.reshape(leading, BLOCKS, PLANES * RX * CY)


def take_blocks(blocked, index_rows):
    return jax.vmap(lambda block_rows, block_index: jnp.take(block_rows, block_index, axis=1), in_axes=(1, 0), out_axes=1)(blocked, index_rows)


def gather_rows(spectrum, skin_cell, live_mask):
    blocked = to_blocks(spectrum.reshape(6 * FREQS, PLANES, NX, NY))
    picked = take_blocks(blocked, skin_cell.reshape(BLOCKS, BLOCKS * CAP))
    return picked.reshape(FREQS, 2, 3, BLOCKS, BLOCKS, CAP) * live_mask


def window_sum(values, along, half_width):
    widths = [(0, 0), (0, 0), (0, 0)]
    widths[along] = (half_width + 1, half_width)
    running = jnp.cumsum(jnp.pad(values, widths), axis=along)
    length = values.shape[along]
    upper_sum = lax.slice_in_dim(running, 2 * half_width, 2 * half_width + length, axis=along)
    lower_sum = lax.slice_in_dim(running, 0, length, axis=along)
    return upper_sum - lower_sum


def reference(e_field, h_field, j_field, material, material_table, dft_e, dft_h, skin_cell, counts, patch_slot, area):
    coeffs = jnp.take(material_table, material, axis=1)
    zero_rows = jnp.zeros((2, PLANES, NY), jnp.float32)
    zero_cols = jnp.zeros((2, PLANES, NX), jnp.float32)
    curl_h = curl_field(h_field, zero_rows, zero_cols)
    e_next = coeffs[0] * e_field + coeffs[1] * (curl_h - j_field)
    j_next = coeffs[2] * j_field + coeffs[3] * (e_next - e_field)
    dft_e_next = accumulate(dft_e, e_next, 0.0)
    dft_h_next = accumulate(dft_h, h_field, 0.5)
    live_mask = (jnp.arange(CAP, dtype=jnp.int32)[None, None, :] < counts[:, :, None]).astype(jnp.float32)
    e_rows = gather_rows(dft_e_next, skin_cell, live_mask)
    h_rows = gather_rows(dft_h_next, skin_cell, live_mask)
    flux = cross_flux(e_rows, h_rows)
    flux = flux.transpose(0, 1, 3, 2, 4).reshape(FREQS, 3, BLOCKS, BLOCKS * CAP)
    area_blocks = area.reshape(3, N_GY, PU, N_GX, PV).transpose(0, 1, 3, 2, 4).reshape(3, BLOCKS, PU * PV)
    patch_index = patch_slot.reshape(BLOCKS, BLOCKS * CAP)
    area_rows = take_blocks(area_blocks, patch_index)
    density = area_rows[0] * flux[:, 0] + area_rows[1] * flux[:, 1] + area_rows[2] * flux[:, 2]
    point_blocks = jax.vmap(lambda target, weight: jnp.zeros((FREQS, PU * PV), jnp.float32).at[:, target].add(weight), in_axes=(0, 1), out_axes=1)(patch_index, density)
    point_density = point_blocks.reshape(FREQS, N_GY, N_GX, PU, PV).transpose(0, 1, 3, 2, 4).reshape(FREQS, U, V)
    strip_sum = window_sum(point_density, 1, HALF)
    avg_density = window_sum(strip_sum, 2, HALF) / (4.0 * HALF * HALF)
    return (e_next, j_next, dft_e_next, dft_h_next, point_density, avg_density)
```

```python
import math

import jax
import jax.numpy as jnp
from jax import lax
from jax.experimental import pallas as pl
from jax.experimental.pallas import tpu as pltpu
from jax.sharding import PartitionSpec as P

STEP = 1000
HALF = 100


FREQ_LIST = (28000000000.0, 39000000000.0, 60000000000.0)
TIME_STEP = 1.9e-13


def shifted(value, axis, steps):
    count = lax.axis_size(axis)
    leading, last = (max(0, -steps), min(count, count - steps))
    return lax.ppermute(value, axis, [(source, source + steps) for source in range(leading, last)])


def with_halo(cells, sides, width):
    for axis, dim in sides:
        count = lax.axis_size(axis)
        ends = count - 1
        head = lax.slice_in_dim(cells, 0, width, axis=dim)
        tail = lax.slice_in_dim(cells, cells.shape[dim] - width, cells.shape[dim], axis=dim)
        cells = jnp.concatenate(
            [
                lax.ppermute(tail, axis, [(i, (i + 1) % count) for i in range(ends)]),
                cells,
                lax.ppermute(head, axis, [((i + 1) % count, i) for i in range(ends)]),
            ],
            axis=dim,
        )
    return cells


def phase_list(offset):
    return [2.0 * math.pi * freq_hz * (STEP + offset) * TIME_STEP for freq_hz in FREQ_LIST]


def shift_of(size):
    return size.bit_length() - 1


def iota0(rows, cols):
    return lax.broadcasted_iota(jnp.int32, (rows, cols), 0)


def split_two(values):
    first = values.astype(jnp.bfloat16)
    return first, (values - first.astype(jnp.float32)).astype(jnp.bfloat16)


def field_kernel(
    h_ref, e_ref, j_ref, mat_ref, table_ref, rows_ref, cols_ref, de_ref, dh_ref,
    en_ref, jn_ref, den_ref, dhn_ref, flux_ref, table_s, cols_s,
):
    step = pl.program_id(0)
    per, rx, cy = mat_ref.shape
    planes = h_ref.shape[1]
    freqs = de_ref.shape[0]
    table_s[...] = jnp.zeros_like(table_s)
    table_s[0:4, 0 : table_ref.shape[1]] = table_ref[...]
    cols_s[...] = jnp.zeros_like(cols_s)
    cols_s[:, 0:rx] = cols_ref[...]
    first_row = iota0(rx, cy) == 0
    first_col = lax.broadcasted_iota(jnp.int32, (rx, cy), 1) == 0
    cos_e = [math.cos(a) for a in phase_list(0.0)]
    sin_e = [-math.sin(a) for a in phase_list(0.0)]
    cos_h = [math.cos(a) for a in phase_list(0.5)]
    sin_h = [-math.sin(a) for a in phase_list(0.5)]

    def row_below(value, comp, z):
        edge = jnp.broadcast_to(rows_ref[comp, pl.ds(z, 1), :], (rx, cy))
        return jnp.where(first_row, edge, pltpu.roll(value, 1, 0))

    def col_below(value, comp, z):
        line = cols_s[pl.ds(comp * planes + z, 1), :]
        edge = jnp.broadcast_to(line, (cy, cy)).T[:rx]
        return jnp.where(first_col, edge, pltpu.roll(value, 1, 1))

    for k in range(per):
        z = step * per + k
        below = jnp.maximum(z - 1, 0)
        keep = jnp.where(z > 0, 1.0, 0.0)
        hx, hy, hz = (h_ref[c, z] for c in range(3))
        curl = (
            (hz - col_below(hz, 1, z)) - (hy - h_ref[1, below] * keep),
            (hx - h_ref[0, below] * keep) - (hz - row_below(hz, 1, z)),
            (hy - row_below(hy, 0, z)) - (hx - col_below(hx, 0, z)),
        )
        kinds = mat_ref[k]
        coeffs = [
            jnp.take_along_axis(
                jnp.broadcast_to(table_s[r : r + 1, :], (rx, cy)), kinds, axis=1,
                mode="promise_in_bounds",
            )
            for r in range(4)
        ]
        en = []
        for c in range(3):
            e_old, j_old = e_ref[c, k], j_ref[c, k]
            e_new = coeffs[0] * e_old + coeffs[1] * (curl[c] - j_old)
            en_ref[c, k] = e_new
            jn_ref[c, k] = coeffs[2] * j_old + coeffs[3] * (e_new - e_old)
            en.append(e_new)
        h_now = (hx, hy, hz)
        for f in range(freqs):
            spectra = []
            for part in range(2):
                e_scale = (cos_e, sin_e)[part][f]
                h_scale = (cos_h, sin_h)[part][f]
                e_part = [de_ref[f, part, c, k] + en[c] * e_scale for c in range(3)]
                h_part = [dh_ref[f, part, c, k] + h_now[c] * h_scale for c in range(3)]
                for c in range(3):
                    den_ref[f, part, c, k] = e_part[c]
                    dhn_ref[f, part, c, k] = h_part[c]
                spectra.append((e_part, h_part))
            for c in range(3):
                a, b = (c + 1) % 3, (c + 2) % 3
                real, imag = [ep[a] * hp[b] - ep[b] * hp[a] for ep, hp in spectra]
                high, low = split_two(0.5 * (real + imag))
                flux_ref[f * 3 + c, k * rx : (k + 1) * rx, 0:cy] = high
                flux_ref[f * 3 + c, k * rx : (k + 1) * rx, cy : 2 * cy] = low


def update_fields(h, e, j, material, table, rows, cols, dft_e, dft_h):
    _, planes, rx, cy = h.shape
    freqs = dft_e.shape[0]
    per = 2 if planes % 2 == 0 else 1
    field_block = pl.BlockSpec((3, per, rx, cy), lambda s: (0, s, 0, 0))
    dft_block = pl.BlockSpec((freqs, 2, 3, per, rx, cy), lambda s: (0, 0, 0, s, 0, 0))
    return pl.pallas_call(
        field_kernel,
        grid=(planes // per,),
        in_specs=[
            pl.BlockSpec(h.shape, lambda s: (0, 0, 0, 0)),
            field_block,
            field_block,
            pl.BlockSpec((per, rx, cy), lambda s: (s, 0, 0)),
            pl.BlockSpec(table.shape, lambda s: (0, 0)),
            pl.BlockSpec(rows.shape, lambda s: (0, 0, 0)),
            pl.BlockSpec(cols.shape, lambda s: (0, 0)),
            dft_block,
            dft_block,
        ],
        out_specs=[
            field_block, field_block, dft_block, dft_block,
            pl.BlockSpec((3 * freqs, per * rx, 2 * cy), lambda s: (0, s, 0)),
        ],
        out_shape=[
            jax.ShapeDtypeStruct(e.shape, jnp.float32),
            jax.ShapeDtypeStruct(j.shape, jnp.float32),
            jax.ShapeDtypeStruct(dft_e.shape, jnp.float32),
            jax.ShapeDtypeStruct(dft_h.shape, jnp.float32),
            jax.ShapeDtypeStruct((3 * freqs, planes * rx, 2 * cy), jnp.bfloat16),
        ],
        scratch_shapes=[
            pltpu.VMEM((8, cy), jnp.float32),
            pltpu.VMEM((2 * planes, cy), jnp.float32),
        ],
        compiler_params=pltpu.CompilerParams(vmem_limit_bytes=40 << 20),
        cost_estimate=pl.CostEstimate(flops=10 * dft_e.size, bytes_accessed=14 << 20, transcendentals=0),
    )(h, e, j, material, table, rows, cols, dft_e, dft_h)


def area_kernel(area_ref, patch_ref, skin_ref, counts_ref, out_ref, live_ref, split_s):
    comps, pu, pv = area_ref.shape
    blocks, cap = patch_ref.shape
    for c in range(comps):
        high, low = split_two(area_ref[c])
        split_s[c, :, 0:pv] = high
        split_s[c, :, pv : 2 * pv] = low
    slots = lax.broadcasted_iota(jnp.int32, (1, cap), 1)

    def pair(t, carry):
        ids = jnp.concatenate([patch_ref[pl.ds(2 * t + i, 1), :] for i in range(2)], 1)
        low = (iota0(pv, 2 * cap) == (ids & (pv - 1))).astype(jnp.float32).astype(jnp.bfloat16)
        both = jnp.concatenate([low, low], 0)
        hit = iota0(pu, 2 * cap) == (ids >> shift_of(pv))
        for c in range(comps):
            rows = jnp.dot(split_s[c], both, preferred_element_type=jnp.float32)
            value = jnp.sum(jnp.where(hit, rows, 0.0), axis=0, keepdims=True)
            for i in range(2):
                out_ref[c, pl.ds(2 * t + i, 1), :] = value[:, i * cap : (i + 1) * cap]
        for i in range(2):
            d = 2 * t + i
            live_ref[pl.ds(d, 1), :] = jnp.where(
                slots < counts_ref[0, d], skin_ref[pl.ds(d, 1), :], -1
            )
        return carry

    lax.fori_loop(0, blocks // 2, pair, 0)


def gather_area(area, patch, skin, counts):
    vmem = pl.BlockSpec(memory_space=pltpu.VMEM)
    blocks, cap = patch.shape
    return pl.pallas_call(
        area_kernel,
        in_specs=[vmem, vmem, vmem, pl.BlockSpec(memory_space=pltpu.SMEM)],
        out_specs=[vmem, vmem],
        out_shape=[
            jax.ShapeDtypeStruct((area.shape[0],) + patch.shape, jnp.float32),
            jax.ShapeDtypeStruct(skin.shape, jnp.int32),
        ],
        scratch_shapes=[
            pltpu.VMEM((area.shape[0], area.shape[1], 2 * area.shape[2]), jnp.bfloat16)
        ],
        compiler_params=pltpu.CompilerParams(vmem_limit_bytes=40 << 20),
        cost_estimate=pl.CostEstimate(
            flops=4 * area.size * blocks * cap, bytes_accessed=4 * area.size, transcendentals=0
        ),
    )(area, patch, skin, counts)


def flux_pair(flux_ref, live_ref, t):
    rows, hi_count, two_lo = flux_ref.shape
    lo_count = two_lo // 2
    ids = jnp.concatenate([live_ref[pl.ds(2 * t + i, 1), :] for i in range(2)], 1)
    width = ids.shape[1]
    low = (iota0(lo_count, width) == (ids & (lo_count - 1))).astype(jnp.float32)
    low = low.astype(jnp.bfloat16)
    both = jnp.concatenate([low, low], 0)
    hit = iota0(hi_count, width) == (ids >> shift_of(lo_count))
    picked = []
    for r in range(rows):
        part = jnp.dot(flux_ref[r], both, preferred_element_type=jnp.float32)
        picked.append(jnp.sum(jnp.where(hit, part, 0.0), axis=0, keepdims=True))
    return picked


def flux_kernel(flux_ref, live_ref, out_ref):
    cap = live_ref.shape[1]

    def pair(t, carry):
        for r, value in enumerate(flux_pair(flux_ref, live_ref, t)):
            for i in range(2):
                out_ref[r, pl.ds(2 * t + i, 1), :] = value[:, i * cap : (i + 1) * cap]
        return carry

    lax.fori_loop(0, live_ref.shape[0] // 2, pair, 0)


def gather_flux(flux, live):
    vmem = pl.BlockSpec(memory_space=pltpu.VMEM)
    return pl.pallas_call(
        flux_kernel,
        in_specs=[vmem, vmem],
        out_specs=vmem,
        out_shape=jax.ShapeDtypeStruct((flux.shape[0],) + live.shape, jnp.float32),
        compiler_params=pltpu.CompilerParams(vmem_limit_bytes=40 << 20),
    )(flux, live)


def spread_kernel(rows_ref, area_ref, patch_ref, out_ref, hi_s, lo_s):
    freqs, pu, pv = out_ref.shape
    blocks, cap = patch_ref.shape
    group = 8
    out_ref[...] = jnp.zeros_like(out_ref)

    def chunk(t, carry):
        here = pl.ds(group * t, group)
        ids = patch_ref[here, :]
        area = [area_ref[c, here, :] for c in range(3)]
        parts = []
        for f in range(freqs):
            dens = area[0] * rows_ref[3 * f, here, :]
            dens = dens + area[1] * rows_ref[3 * f + 1, here, :]
            dens = dens + area[2] * rows_ref[3 * f + 2, here, :]
            high = dens.astype(jnp.bfloat16).astype(jnp.float32)
            parts.append((high, dens - high))
        for i in range(group):
            lanes = slice(i * cap, (i + 1) * cap)
            row = ids[i : i + 1]
            hi_hit = iota0(pu, cap) == (row >> shift_of(pv))
            hi_s[:, lanes] = hi_hit.astype(jnp.float32).astype(jnp.bfloat16)
            lo_hit = iota0(pv, cap) == (row & (pv - 1))
            for f in range(freqs):
                for p in range(2):
                    lo_s[f, p, :, lanes] = jnp.where(
                        lo_hit, parts[f][p][i : i + 1], 0.0
                    ).astype(jnp.bfloat16)
        nt = (((1,), (1,)), ((), ()))
        for f in range(freqs):
            out_ref[f] += lax.dot_general(
                hi_s[...], lo_s[f, 0], nt, preferred_element_type=jnp.float32
            ) + lax.dot_general(hi_s[...], lo_s[f, 1], nt, preferred_element_type=jnp.float32)
        return carry

    lax.fori_loop(0, blocks // group, chunk, 0)


def spread(rows, area_rows, patch, pu, pv):
    vmem = pl.BlockSpec(memory_space=pltpu.VMEM)
    freqs = rows.shape[0] // 3
    width = 8 * patch.shape[1]
    return pl.pallas_call(
        spread_kernel,
        in_specs=[vmem] * 3,
        out_specs=vmem,
        out_shape=jax.ShapeDtypeStruct((freqs, pu, pv), jnp.float32),
        scratch_shapes=[
            pltpu.VMEM((pu, width), jnp.bfloat16),
            pltpu.VMEM((freqs, 2, pv, width), jnp.bfloat16),
        ],
        compiler_params=pltpu.CompilerParams(vmem_limit_bytes=40 << 20),
    )(rows, area_rows, patch)


def band_matrix(count, half_width):
    row_ids = lax.broadcasted_iota(jnp.int32, (count, count + 2 * half_width), 0)
    col_ids = lax.broadcasted_iota(jnp.int32, (count, count + 2 * half_width), 1)
    return ((col_ids >= row_ids) & (col_ids < row_ids + 2 * half_width)).astype(jnp.float32)


def shards(
    e_field, h_field, j_field, material, material_table, dft_e, dft_h, skin_cell, counts,
    patch_slot, area,
):
    planes, rx = h_field.shape[1:3]
    rows_below = shifted(h_field[1:3, :, -1, :], "gy", 1)
    cols_left = shifted(h_field[0::2, :, :, -1].reshape(2 * planes, rx), "gx", 1)
    blocks, cap = skin_cell.shape[1:]
    patch = patch_slot.reshape(blocks, cap)
    area_rows, live = gather_area(area, patch, skin_cell.reshape(blocks, cap), counts)
    e_next, j_next, dft_e_next, dft_h_next, flux = update_fields(
        h_field, e_field, j_field, material, material_table, rows_below, cols_left, dft_e, dft_h
    )
    arrived = lax.all_to_all(
        gather_flux(flux, live), ("gy", "gx"), split_axis=1, concat_axis=1, tiled=True
    )
    rows_u, cols_v = area.shape[1:]
    point_density = spread(arrived, area_rows, patch, rows_u, cols_v)
    padded = with_halo(point_density, (("gy", 1),), HALF)
    strip_sum = jnp.einsum(
        "ij,fjv->fiv",
        band_matrix(rows_u, HALF),
        padded,
        precision=lax.Precision.HIGHEST,
        preferred_element_type=jnp.float32,
    )
    padded_cols = with_halo(strip_sum, (("gx", 2),), HALF)
    square_sum = jnp.einsum(
        "fuj,ij->fui",
        padded_cols,
        band_matrix(cols_v, HALF),
        precision=lax.Precision.HIGHEST,
        preferred_element_type=jnp.float32,
    )
    avg_density = square_sum / (4.0 * HALF * HALF)
    return (e_next, j_next, dft_e_next, dft_h_next, point_density, avg_density)


def solution(mesh):
    placed = (
        P(None, None, "gy", "gx"),
        P(None, None, "gy", "gx"),
        P(None, None, "gy", "gx"),
        P(None, "gy", "gx"),
        P(),
        P(None, None, None, None, "gy", "gx"),
        P(None, None, None, None, "gy", "gx"),
        P(("gy", "gx"), None, None),
        P(("gy", "gx"), None),
        P(("gy", "gx"), None, None),
        P(None, "gy", "gx"),
    )
    return jax.shard_map(
        shards,
        mesh=mesh,
        in_specs=placed,
        out_specs=(
            P(None, None, "gy", "gx"),
            P(None, None, "gy", "gx"),
            P(None, None, None, None, "gy", "gx"),
            P(None, None, None, None, "gy", "gx"),
            P(None, "gy", "gx"),
            P(None, "gy", "gx"),
        ),
        check_vma=False,
    )
```

```python
import math

import jax
import jax.numpy as jnp
from jax import lax
from jax.experimental import pallas as pl
from jax.experimental.pallas import tpu as pltpu
from jax.sharding import PartitionSpec as P

STEP = 1000
HALF = 100


FREQ_LIST = (28000000000.0, 39000000000.0, 60000000000.0)
TIME_STEP = 1.9e-13


MESH = pl.DeviceIdType.MESH


def phase_list(offset):
    return [2.0 * math.pi * freq_hz * (STEP + offset) * TIME_STEP for freq_hz in FREQ_LIST]


def shift_of(size):
    return size.bit_length() - 1


def iota0(rows, cols):
    return lax.broadcasted_iota(jnp.int32, (rows, cols), 0)


def split_two(values):
    first = values.astype(jnp.bfloat16)
    return first, (values - first.astype(jnp.float32)).astype(jnp.bfloat16)


def field_kernel(
    h_ref, e_ref, j_ref, mat_ref, table_ref, rows_ref, cols_ref, de_ref, dh_ref,
    en_ref, jn_ref, den_ref, dhn_ref, flux_ref, table_s,
):
    step = pl.program_id(0)
    per, rx, cy = mat_ref.shape
    planes = h_ref.shape[1]
    freqs = de_ref.shape[0]
    table_s[...] = jnp.zeros_like(table_s)
    table_s[0:4, 0 : table_ref.shape[1]] = table_ref[...]
    first_row = iota0(rx, cy) == 0
    first_col = lax.broadcasted_iota(jnp.int32, (rx, cy), 1) == 0
    cos_e = [math.cos(a) for a in phase_list(0.0)]
    sin_e = [-math.sin(a) for a in phase_list(0.0)]
    cos_h = [math.cos(a) for a in phase_list(0.5)]
    sin_h = [-math.sin(a) for a in phase_list(0.5)]

    def row_below(value, comp, z):
        edge = jnp.broadcast_to(rows_ref[pl.ds(comp * planes + z, 1), :], (rx, cy))
        return jnp.where(first_row, edge, pltpu.roll(value, 1, 0))

    def col_below(value, comp, z):
        line = cols_ref[pl.ds(comp * planes + z, 1), :]
        edge = jnp.broadcast_to(line, (cy, cy)).T[:rx]
        return jnp.where(first_col, edge, pltpu.roll(value, 1, 1))

    for k in range(per):
        z = step * per + k
        below = jnp.maximum(z - 1, 0)
        keep = jnp.where(z > 0, 1.0, 0.0)
        hx, hy, hz = (h_ref[c, z] for c in range(3))
        curl = (
            (hz - col_below(hz, 1, z)) - (hy - h_ref[1, below] * keep),
            (hx - h_ref[0, below] * keep) - (hz - row_below(hz, 1, z)),
            (hy - row_below(hy, 0, z)) - (hx - col_below(hx, 0, z)),
        )
        kinds = mat_ref[k]
        coeffs = [
            jnp.take_along_axis(
                jnp.broadcast_to(table_s[r : r + 1, :], (rx, cy)), kinds, axis=1,
                mode="promise_in_bounds",
            )
            for r in range(4)
        ]
        en = []
        for c in range(3):
            e_old, j_old = e_ref[c, k], j_ref[c, k]
            e_new = coeffs[0] * e_old + coeffs[1] * (curl[c] - j_old)
            en_ref[c, k] = e_new
            jn_ref[c, k] = coeffs[2] * j_old + coeffs[3] * (e_new - e_old)
            en.append(e_new)
        h_now = (hx, hy, hz)
        for f in range(freqs):
            spectra = []
            for part in range(2):
                e_scale = (cos_e, sin_e)[part][f]
                h_scale = (cos_h, sin_h)[part][f]
                e_part = [de_ref[f, part, c, k] + en[c] * e_scale for c in range(3)]
                h_part = [dh_ref[f, part, c, k] + h_now[c] * h_scale for c in range(3)]
                for c in range(3):
                    den_ref[f, part, c, k] = e_part[c]
                    dhn_ref[f, part, c, k] = h_part[c]
                spectra.append((e_part, h_part))
            for c in range(3):
                a, b = (c + 1) % 3, (c + 2) % 3
                real, imag = [ep[a] * hp[b] - ep[b] * hp[a] for ep, hp in spectra]
                high, low = split_two(0.5 * (real + imag))
                flux_ref[f * 3 + c, k * rx : (k + 1) * rx, 0:cy] = high
                flux_ref[f * 3 + c, k * rx : (k + 1) * rx, cy : 2 * cy] = low


def update_fields(h, e, j, material, table, rows, cols, dft_e, dft_h):
    _, planes, rx, cy = h.shape
    freqs = dft_e.shape[0]
    per = 2 if planes % 2 == 0 else 1
    field_block = pl.BlockSpec((3, per, rx, cy), lambda s: (0, s, 0, 0))
    dft_block = pl.BlockSpec((freqs, 2, 3, per, rx, cy), lambda s: (0, 0, 0, s, 0, 0))
    return pl.pallas_call(
        field_kernel,
        grid=(planes // per,),
        in_specs=[
            pl.BlockSpec(h.shape, lambda s: (0, 0, 0, 0)),
            field_block,
            field_block,
            pl.BlockSpec((per, rx, cy), lambda s: (s, 0, 0)),
            pl.BlockSpec(table.shape, lambda s: (0, 0)),
            pl.BlockSpec(rows.shape, lambda s: (0, 0)),
            pl.BlockSpec(cols.shape, lambda s: (0, 0)),
            dft_block,
            dft_block,
        ],
        out_specs=[
            field_block, field_block, dft_block, dft_block,
            pl.BlockSpec((3 * freqs, per * rx, 2 * cy), lambda s: (0, s, 0)),
        ],
        out_shape=[
            jax.ShapeDtypeStruct(e.shape, jnp.float32),
            jax.ShapeDtypeStruct(j.shape, jnp.float32),
            jax.ShapeDtypeStruct(dft_e.shape, jnp.float32),
            jax.ShapeDtypeStruct(dft_h.shape, jnp.float32),
            jax.ShapeDtypeStruct((3 * freqs, planes * rx, 2 * cy), jnp.bfloat16),
        ],
        scratch_shapes=[pltpu.VMEM((8, cy), jnp.float32)],
        compiler_params=pltpu.CompilerParams(vmem_limit_bytes=40 << 20),
        cost_estimate=pl.CostEstimate(flops=10 * dft_e.size, bytes_accessed=14 << 20, transcendentals=0),
    )(h, e, j, material, table, rows, cols, dft_e, dft_h)


def signal(sem, where):
    pl.semaphore_signal(sem, inc=1, device_id=where, device_id_type=MESH)


def remote(src, dst, send_sem, recv_sem, where):
    return pltpu.make_async_remote_copy(
        src_ref=src, dst_ref=dst, send_sem=send_sem, recv_sem=recv_sem,
        device_id=where, device_id_type=MESH,
    )


def area_kernel(
    h_any, area_any, patch_ref, skin_ref, counts_ref,
    out_ref, live_ref, rows_ref, cols_ref,
    h_s, area_s, split_s, row_edge, col_edge, load_sem, send_sem, recv_sem,
):
    comps, pu, pv = area_s.shape
    blocks, cap = patch_ref.shape
    _, planes, rx, cy = h_s.shape
    axes = ("gy", "gx")
    place = [lax.axis_index(axis) for axis in axes]
    count = [lax.axis_size(axis) for axis in axes]
    h_load = pltpu.make_async_copy(h_any, h_s, load_sem.at[0])
    area_load = pltpu.make_async_copy(area_any, area_s, load_sem.at[1])
    h_load.start()
    area_load.start()
    barrier = pltpu.get_barrier_semaphore()
    for axis, at in zip(axes, place):

        @pl.when(at > 0)
        def _():
            signal(barrier, {axis: at - 1})

    h_load.wait()
    col_edge[...] = jnp.zeros_like(col_edge)
    for k in range(2):
        for z in range(planes):
            line = k * planes + z
            row_edge[line : line + 1, :] = h_s[1 + k, z, rx - 1 : rx, :]
            col_edge[line : line + 1, 0:rx] = h_s[2 * k, z].T[cy - 1 : cy, :]
    edges = (row_edge, col_edge)
    landing = (rows_ref, cols_ref)
    copies = [
        remote(edges[i], landing[i], send_sem.at[i], recv_sem.at[i], {axes[i]: place[i] + 1})
        for i in range(2)
    ]
    peers = sum(jnp.where(at < size - 1, 1, 0) for at, size in zip(place, count))

    @pl.when(peers > 0)
    def _():
        pl.semaphore_wait(barrier, peers)

    for i in range(2):

        @pl.when(place[i] < count[i] - 1)
        def _():
            copies[i].start()

        @pl.when(place[i] == 0)
        def _():
            landing[i][...] = jnp.zeros_like(landing[i])

    area_load.wait()
    for c in range(comps):
        high, low = split_two(area_s[c])
        split_s[c, :, 0:pv] = high
        split_s[c, :, pv : 2 * pv] = low
    slots = lax.broadcasted_iota(jnp.int32, (1, cap), 1)

    def one_group(t, carry):
        for q in range(4):
            first = 8 * t + 2 * q
            ids = jnp.concatenate([patch_ref[pl.ds(first + i, 1), :] for i in range(2)], 1)
            low = (iota0(pv, 2 * cap) == (ids & (pv - 1))).astype(jnp.float32)
            low = low.astype(jnp.bfloat16)
            both = jnp.concatenate([low, low], 0)
            hit = iota0(pu, 2 * cap) == (ids >> shift_of(pv))
            for c in range(comps):
                rows = jnp.dot(split_s[c], both, preferred_element_type=jnp.float32)
                value = jnp.sum(jnp.where(hit, rows, 0.0), axis=0, keepdims=True)
                for i in range(2):
                    out_ref[c, pl.ds(first + i, 1), :] = value[:, i * cap : (i + 1) * cap]
        here = pl.ds(pl.multiple_of(8 * t, 8), 8)
        live_ref[here, :] = jnp.where(slots < counts_ref[here, :], skin_ref[here, :], -1)
        return carry

    lax.fori_loop(0, blocks // 8, one_group, 0)
    for i in range(2):

        @pl.when(place[i] < count[i] - 1)
        def _():
            copies[i].wait_send()

        @pl.when(place[i] > 0)
        def _():
            copies[i].wait_recv()


def gather_area(h, area, patch, skin, counts):
    vmem = pl.BlockSpec(memory_space=pltpu.VMEM)
    blocks, cap = patch.shape
    _, planes, rx, cy = h.shape
    edge = (2 * planes, cy)
    return pl.pallas_call(
        area_kernel,
        in_specs=[pl.BlockSpec(memory_space=pl.ANY)] * 2 + [vmem] * 3,
        out_specs=[vmem] * 4,
        out_shape=[
            jax.ShapeDtypeStruct((area.shape[0],) + patch.shape, jnp.float32),
            jax.ShapeDtypeStruct(skin.shape, jnp.int32),
            jax.ShapeDtypeStruct(edge, jnp.float32),
            jax.ShapeDtypeStruct(edge, jnp.float32),
        ],
        scratch_shapes=[
            pltpu.VMEM(h.shape, jnp.float32),
            pltpu.VMEM(area.shape, jnp.float32),
            pltpu.VMEM((area.shape[0], area.shape[1], 2 * area.shape[2]), jnp.bfloat16),
            pltpu.VMEM(edge, jnp.float32),
            pltpu.VMEM(edge, jnp.float32),
            pltpu.SemaphoreType.DMA((2,)),
            pltpu.SemaphoreType.DMA((2,)),
            pltpu.SemaphoreType.DMA((2,)),
        ],
        compiler_params=pltpu.CompilerParams(
            vmem_limit_bytes=40 << 20, collective_id=0, has_side_effects=True
        ),
    )(h, area, patch, skin, counts)


def flux_pair(flux_ref, live_ref, t):
    rows, hi_count, two_lo = flux_ref.shape
    lo_count = two_lo // 2
    ids = jnp.concatenate([live_ref[pl.ds(2 * t + i, 1), :] for i in range(2)], 1)
    width = ids.shape[1]
    low = (iota0(lo_count, width) == (ids & (lo_count - 1))).astype(jnp.float32)
    low = low.astype(jnp.bfloat16)
    both = jnp.concatenate([low, low], 0)
    hit = iota0(hi_count, width) == (ids >> shift_of(lo_count))
    picked = []
    for r in range(rows):
        part = jnp.dot(flux_ref[r], both, preferred_element_type=jnp.float32)
        picked.append(jnp.sum(jnp.where(hit, part, 0.0), axis=0, keepdims=True))
    return picked


def flux_kernel(flux_ref, live_ref, out_ref, pack_s, send_sem, recv_sem):
    blocks, cap = live_ref.shape
    n_gx = lax.axis_size("gx")
    me = lax.axis_index("gy") * n_gx + lax.axis_index("gx")
    groups = blocks // 8
    barrier = pltpu.get_barrier_semaphore()

    def greet(k, carry):
        d = (me + k) % blocks
        signal(barrier, (d // n_gx, d % n_gx))
        return carry

    lax.fori_loop(1, blocks, greet, 0)

    def gather_group(step):
        group = (me // 8 + step) % groups
        for q in range(4):
            picked = flux_pair(flux_ref, live_ref, group * 4 + q)
            for r, value in enumerate(picked):
                for i in range(2):
                    pack_s[group * 8 + 2 * q + i, r : r + 1, :] = value[:, i * cap : (i + 1) * cap]
        return group

    def copy_to(d):
        return remote(
            pack_s.at[d], out_ref.at[me], send_sem.at[d], recv_sem.at[me],
            (d // n_gx, d % n_gx),
        )

    def send_group(group):
        def send_one(i, carry):
            d = group * 8 + i

            @pl.when(d != me)
            def _():
                copy_to(d).start()

            return carry

        lax.fori_loop(0, 8, send_one, 0)

    own = gather_group(0)
    out_ref[me] = pack_s[me]
    pl.semaphore_wait(barrier, blocks - 1)
    send_group(own)

    def one_step(step, carry):
        send_group(gather_group(step))
        return carry

    lax.fori_loop(1, groups, one_step, 0)

    def finish(k, carry):
        d = (me + k) % blocks
        copy_to(d).wait_send()
        remote(
            pack_s.at[d], out_ref.at[d], send_sem.at[d], recv_sem.at[d],
            (d // n_gx, d % n_gx),
        ).wait_recv()
        return carry

    lax.fori_loop(1, blocks, finish, 0)


def exchange_flux(flux, live):
    vmem = pl.BlockSpec(memory_space=pltpu.VMEM)
    blocks, cap = live.shape
    shape = (blocks, flux.shape[0], cap)
    return pl.pallas_call(
        flux_kernel,
        in_specs=[vmem, vmem],
        out_specs=vmem,
        out_shape=jax.ShapeDtypeStruct(shape, jnp.float32),
        scratch_shapes=[
            pltpu.VMEM(shape, jnp.float32),
            pltpu.SemaphoreType.DMA((blocks,)),
            pltpu.SemaphoreType.DMA((blocks,)),
        ],
        compiler_params=pltpu.CompilerParams(
            vmem_limit_bytes=40 << 20, collective_id=1, has_side_effects=True
        ),
    )(flux, live)


NT = (((1,), (1,)), ((), ()))
REACH = 104
PAD = 128


def band_kernel(
    rows_ref, area_ref, patch_ref, point_ref, avg_ref,
    dens_s, side_dens, side_patch, hi_own, hi_side, strip_s,
    send_sem, recv_sem, u_send, u_recv,
):
    freqs, pu, pv = point_ref.shape
    blocks, cap = patch_ref.shape
    gy, gx = lax.axis_index("gy"), lax.axis_index("gx")
    n_gy, n_gx = lax.axis_size("gy"), lax.axis_size("gx")
    sides = [("gx", gx > 0, gx - 1), ("gx", gx < n_gx - 1, gx + 1)]
    ends = [("gy", gy > 0, gy - 1), ("gy", gy < n_gy - 1, gy + 1)]
    barrier = pltpu.get_barrier_semaphore()
    for axis, there, at in sides + ends:

        @pl.when(there)
        def _():
            signal(barrier, {axis: at})

    for f in range(freqs):
        dens = area_ref[0] * rows_ref[:, 3 * f, :]
        dens = dens + area_ref[1] * rows_ref[:, 3 * f + 1, :]
        dens_s[f] = dens + area_ref[2] * rows_ref[:, 3 * f + 2, :]
    pl.semaphore_wait(barrier, sum(jnp.where(there, 1, 0) for _, there, _ in sides + ends))
    side_copies = []
    for i, (axis, there, at) in enumerate(sides):
        copies = [
            remote(dens_s, side_dens.at[1 - i], send_sem.at[i, 0], recv_sem.at[1 - i, 0], {axis: at}),
            remote(patch_ref, side_patch.at[1 - i], send_sem.at[i, 1], recv_sem.at[1 - i, 1], {axis: at}),
        ]
        arrivals = [
            remote(dens_s, side_dens.at[i], send_sem.at[i, 0], recv_sem.at[i, 0], {axis: at}),
            remote(patch_ref, side_patch.at[i], send_sem.at[i, 1], recv_sem.at[i, 1], {axis: at}),
        ]
        side_copies.append((there, copies, arrivals))

        @pl.when(there)
        def _():
            for copy in copies:
                copy.start()

        @pl.when(jnp.logical_not(there))
        def _():
            side_dens[i] = jnp.zeros_like(side_dens.at[i])
            side_patch[i] = jnp.zeros_like(side_patch.at[i])

    strip_s[:, 0 : PAD - REACH, :] = jnp.zeros((freqs, PAD - REACH, pv), jnp.float32)
    strip_s[:, pu + PAD + REACH :, :] = jnp.zeros((freqs, PAD - REACH, pv), jnp.float32)
    landing = [pl.ds(PAD - REACH, REACH), pl.ds(PAD + pu, REACH)]
    leaving = [pl.ds(PAD, REACH), pl.ds(PAD + pu - REACH, REACH)]
    for i, (axis, there, at) in enumerate(ends):

        @pl.when(jnp.logical_not(there))
        def _():
            strip_s[:, landing[i], :] = jnp.zeros((freqs, REACH, pv), jnp.float32)

    group = 32 if blocks % 32 == 0 else blocks
    groups = blocks // group

    def rows_of(ids, i):
        return ids[i : i + 1]

    def hi_part(ids, size):
        pieces = [
            (iota0(size, cap) == (rows_of(ids, i) >> shift_of(pv))).astype(jnp.float32)
            for i in range(group)
        ]
        return jnp.concatenate(pieces, 1).astype(jnp.bfloat16)

    def own_step(f, t):
        here = pl.ds(pl.multiple_of(t * group, 8), group)
        ids = patch_ref[here, :]
        if f == 0:
            hi = hi_part(ids, pu)
            hi_own[t] = hi
        else:
            hi = hi_own[t]
        dens = dens_s[f, here, :]
        first = dens.astype(jnp.bfloat16).astype(jnp.float32)
        out = None
        hits = [iota0(pv, cap) == (rows_of(ids, i) & (pv - 1)) for i in range(group)]
        for part in (first, dens - first):
            spread = jnp.concatenate(
                [
                    jnp.where(hits[i], rows_of(part, i), 0.0).astype(jnp.bfloat16)
                    for i in range(group)
                ],
                1,
            )
            one = lax.dot_general(hi, spread, NT, preferred_element_type=jnp.float32)
            out = one if out is None else out + one
        return out

    def own(f):
        point_ref[f] = own_step(f, 0)

        def more(t, carry):
            point_ref[f] += own_step(f, t)
            return carry

        if groups > 1:
            lax.fori_loop(1, groups, more, 0)

    half = pv // 2

    def side_step(f, i, t):
        here = pl.ds(pl.multiple_of(t * group, 8), group)
        ids = side_patch[i, here, :]
        if f == 0:
            hi = hi_part(ids, pu)
            hi_side[i, t] = hi
        else:
            hi = hi_side[i, t]
        dens = side_dens[i, f, here, :]
        first = dens.astype(jnp.bfloat16).astype(jnp.float32)
        rest = dens - first
        pieces = []
        for s in range(group):
            cell = rows_of(ids, s) & (pv - 1)
            if i == 0:
                within = cell >= iota0(half, cap) + (pv - HALF)
            else:
                within = cell <= iota0(half, cap) + (half - 1 - pv + HALF)
            pieces.append(
                jnp.concatenate(
                    [jnp.where(within, rows_of(part, s), 0.0) for part in (first, rest)], 0
                ).astype(jnp.bfloat16)
            )
        out = lax.dot_general(
            hi, jnp.concatenate(pieces, 1), NT, preferred_element_type=jnp.float32
        )
        return out[:, :half] + out[:, half:]

    rows_at = pl.ds(PAD, pu)

    def strip(f):
        k, v = iota0(pv, pv), lax.broadcasted_iota(jnp.int32, (pv, pv), 1)
        band = ((k >= v - HALF) & (k < v + HALF)).astype(jnp.float32).astype(jnp.bfloat16)
        high, low = split_two(point_ref[f])
        mid = jnp.dot(high, band, preferred_element_type=jnp.float32)
        mid = mid + jnp.dot(low, band, preferred_element_type=jnp.float32)
        strip_s[f, rows_at, 0:half] = mid[:, :half] + side_step(f, 0, 0)
        strip_s[f, rows_at, half:pv] = mid[:, half:] + side_step(f, 1, 0)

        def more(t, carry):
            strip_s[f, rows_at, 0:half] += side_step(f, 0, t)
            strip_s[f, rows_at, half:pv] += side_step(f, 1, t)
            return carry

        if groups > 1:
            lax.fori_loop(1, groups, more, 0)

    def end_copy(f, i, arrival):
        axis, there, at = ends[i]
        lands = i if arrival else 1 - i
        return remote(
            strip_s.at[f, leaving[i]], strip_s.at[f, landing[lands]],
            u_send.at[f, i], u_recv.at[f, lands], {axis: at},
        )

    def send_ends(f):
        for i, (axis, there, at) in enumerate(ends):

            @pl.when(there)
            def _():
                end_copy(f, i, False).start()

    def average(f):
        for i, (axis, there, at) in enumerate(ends):

            @pl.when(there)
            def _():
                end_copy(f, i, True).wait_recv()

        u = iota0(pu, pu + 2 * PAD)
        g = lax.broadcasted_iota(jnp.int32, (pu, pu + 2 * PAD), 1) - PAD
        band = ((g >= u - HALF) & (g < u + HALF)).astype(jnp.float32).astype(jnp.bfloat16)
        high, low = split_two(strip_s[f])
        total = jnp.dot(band, high, preferred_element_type=jnp.float32)
        total = total + jnp.dot(band, low, preferred_element_type=jnp.float32)
        avg_ref[f] = total * (1.0 / (4.0 * HALF * HALF))

    own(0)
    own(1)
    for there, copies, arrivals in side_copies:

        @pl.when(there)
        def _():
            for copy in arrivals:
                copy.wait_recv()

    strip(0)
    send_ends(0)
    own(2)
    strip(1)
    send_ends(1)
    strip(2)
    send_ends(2)
    for f in range(freqs):
        average(f)
    for there, copies, arrivals in side_copies:

        @pl.when(there)
        def _():
            for copy in copies:
                copy.wait_send()

    for f in range(freqs):
        for i, (axis, there, at) in enumerate(ends):

            @pl.when(there)
            def _():
                end_copy(f, i, False).wait_send()


def surface(rows, area_rows, patch, pu, pv):
    vmem = pl.BlockSpec(memory_space=pltpu.VMEM)
    blocks, cap = patch.shape
    freqs = rows.shape[1] // 3
    group = 32 if blocks % 32 == 0 else blocks
    out = jax.ShapeDtypeStruct((freqs, pu, pv), jnp.float32)
    return pl.pallas_call(
        band_kernel,
        in_specs=[vmem] * 3,
        out_specs=[vmem] * 2,
        out_shape=[out, out],
        scratch_shapes=[
            pltpu.VMEM((freqs, blocks, cap), jnp.float32),
            pltpu.VMEM((2, freqs, blocks, cap), jnp.float32),
            pltpu.VMEM((2, blocks, cap), jnp.int32),
            pltpu.VMEM((blocks // group, pu, group * cap), jnp.bfloat16),
            pltpu.VMEM((2, blocks // group, pu, group * cap), jnp.bfloat16),
            pltpu.VMEM((freqs, pu + 2 * PAD, pv), jnp.float32),
            pltpu.SemaphoreType.DMA((2, 2)),
            pltpu.SemaphoreType.DMA((2, 2)),
            pltpu.SemaphoreType.DMA((freqs, 2)),
            pltpu.SemaphoreType.DMA((freqs, 2)),
        ],
        compiler_params=pltpu.CompilerParams(
            vmem_limit_bytes=52 << 20, collective_id=2, has_side_effects=True
        ),
    )(rows, area_rows, patch)


def shards(
    e_field, h_field, j_field, material, material_table, dft_e, dft_h, skin_cell, counts,
    patch_slot, area,
):
    blocks, cap = skin_cell.shape[1:]
    patch = patch_slot.reshape(blocks, cap)
    area_rows, live, rows_below, cols_left = gather_area(
        h_field, area, patch, skin_cell.reshape(blocks, cap), counts.reshape(blocks, 1)
    )
    e_next, j_next, dft_e_next, dft_h_next, flux = update_fields(
        h_field, e_field, j_field, material, material_table, rows_below, cols_left, dft_e, dft_h
    )
    arrived = exchange_flux(flux, live)
    point_density, avg_density = surface(arrived, area_rows, patch, area.shape[1], area.shape[2])
    return (e_next, j_next, dft_e_next, dft_h_next, point_density, avg_density)


def solution(mesh):
    placed = (
        P(None, None, "gy", "gx"),
        P(None, None, "gy", "gx"),
        P(None, None, "gy", "gx"),
        P(None, "gy", "gx"),
        P(),
        P(None, None, None, None, "gy", "gx"),
        P(None, None, None, None, "gy", "gx"),
        P(("gy", "gx"), None, None),
        P(("gy", "gx"), None),
        P(("gy", "gx"), None, None),
        P(None, "gy", "gx"),
    )
    return jax.shard_map(
        shards,
        mesh=mesh,
        in_specs=placed,
        out_specs=(
            P(None, None, "gy", "gx"),
            P(None, None, "gy", "gx"),
            P(None, None, None, None, "gy", "gx"),
            P(None, None, None, None, "gy", "gx"),
            P(None, "gy", "gx"),
            P(None, "gy", "gx"),
        ),
        check_vma=False,
    )
```

```python
import math

import jax
import jax.numpy as jnp
from jax import lax
from jax.experimental import pallas as pl
from jax.experimental.pallas import tpu as pltpu
from jax.sharding import PartitionSpec as P

STEP = 1000
HALF = 100


FREQ_LIST = (28000000000.0, 39000000000.0, 60000000000.0)
TIME_STEP = 1.9e-13


VMEM_ALL = (64 << 20) - (256 << 10)
MESH = pl.DeviceIdType.MESH


def phase_list(offset):
    return [2.0 * math.pi * freq_hz * (STEP + offset) * TIME_STEP for freq_hz in FREQ_LIST]


def shift_of(size):
    return size.bit_length() - 1


def iota0(rows, cols):
    return lax.broadcasted_iota(jnp.int32, (rows, cols), 0)


def split_two(values):
    first = values.astype(jnp.bfloat16)
    return first, (values - first.astype(jnp.float32)).astype(jnp.bfloat16)


def field_kernel(
    h_ref, e_ref, j_ref, mat_ref, table_ref, rows_ref, cols_ref, de_ref, dh_ref,
    en_ref, jn_ref, den_ref, dhn_ref, flux_ref, table_s,
):
    step = pl.program_id(0)
    per, rx, cy = mat_ref.shape
    planes = h_ref.shape[1]
    freqs = de_ref.shape[0]
    table_s[...] = jnp.zeros_like(table_s)
    table_s[0:4, 0 : table_ref.shape[1]] = table_ref[...]
    first_row = iota0(rx, cy) == 0
    first_col = lax.broadcasted_iota(jnp.int32, (rx, cy), 1) == 0
    cos_e = [math.cos(a) for a in phase_list(0.0)]
    sin_e = [-math.sin(a) for a in phase_list(0.0)]
    cos_h = [math.cos(a) for a in phase_list(0.5)]
    sin_h = [-math.sin(a) for a in phase_list(0.5)]

    def row_below(value, comp, z):
        edge = jnp.broadcast_to(rows_ref[pl.ds(comp * planes + z, 1), :], (rx, cy))
        return jnp.where(first_row, edge, pltpu.roll(value, 1, 0))

    def col_below(value, comp, z):
        line = cols_ref[pl.ds(comp * planes + z, 1), :]
        edge = jnp.broadcast_to(line, (cy, cy)).T[:rx]
        return jnp.where(first_col, edge, pltpu.roll(value, 1, 1))

    for k in range(per):
        z = step * per + k
        below = jnp.maximum(z - 1, 0)
        keep = jnp.where(z > 0, 1.0, 0.0)
        hx, hy, hz = (h_ref[c, z] for c in range(3))
        curl = (
            (hz - col_below(hz, 1, z)) - (hy - h_ref[1, below] * keep),
            (hx - h_ref[0, below] * keep) - (hz - row_below(hz, 1, z)),
            (hy - row_below(hy, 0, z)) - (hx - col_below(hx, 0, z)),
        )
        kinds = mat_ref[k]
        coeffs = [
            jnp.take_along_axis(
                jnp.broadcast_to(table_s[r : r + 1, :], (rx, cy)), kinds, axis=1,
                mode="promise_in_bounds",
            )
            for r in range(4)
        ]
        en = []
        for c in range(3):
            e_old, j_old = e_ref[c, k], j_ref[c, k]
            e_new = coeffs[0] * e_old + coeffs[1] * (curl[c] - j_old)
            en_ref[c, k] = e_new
            jn_ref[c, k] = coeffs[2] * j_old + coeffs[3] * (e_new - e_old)
            en.append(e_new)
        h_now = (hx, hy, hz)
        for f in range(freqs):
            spectra = []
            for part in range(2):
                e_scale = (cos_e, sin_e)[part][f]
                h_scale = (cos_h, sin_h)[part][f]
                e_part = [de_ref[f, part, c, k] + en[c] * e_scale for c in range(3)]
                h_part = [dh_ref[f, part, c, k] + h_now[c] * h_scale for c in range(3)]
                for c in range(3):
                    den_ref[f, part, c, k] = e_part[c]
                    dhn_ref[f, part, c, k] = h_part[c]
                spectra.append((e_part, h_part))
            for c in range(3):
                a, b = (c + 1) % 3, (c + 2) % 3
                real, imag = [ep[a] * hp[b] - ep[b] * hp[a] for ep, hp in spectra]
                high, low = split_two(0.5 * (real + imag))
                flux_ref[f * 3 + c, k * rx : (k + 1) * rx, 0:cy] = high
                flux_ref[f * 3 + c, k * rx : (k + 1) * rx, cy : 2 * cy] = low


def update_fields(h, e, j, material, table, rows, cols, dft_e, dft_h):
    _, planes, rx, cy = h.shape
    freqs = dft_e.shape[0]
    per = 2 if planes % 2 == 0 else 1
    field_block = pl.BlockSpec((3, per, rx, cy), lambda s: (0, s, 0, 0))
    dft_block = pl.BlockSpec((freqs, 2, 3, per, rx, cy), lambda s: (0, 0, 0, s, 0, 0))
    return pl.pallas_call(
        field_kernel,
        grid=(planes // per,),
        in_specs=[
            pl.BlockSpec(h.shape, lambda s: (0, 0, 0, 0)),
            field_block,
            field_block,
            pl.BlockSpec((per, rx, cy), lambda s: (s, 0, 0)),
            pl.BlockSpec(table.shape, lambda s: (0, 0)),
            pl.BlockSpec(rows.shape, lambda s: (0, 0)),
            pl.BlockSpec(cols.shape, lambda s: (0, 0)),
            dft_block,
            dft_block,
        ],
        out_specs=[
            field_block, field_block, dft_block, dft_block,
            pl.BlockSpec((3 * freqs, per * rx, 2 * cy), lambda s: (0, s, 0)),
        ],
        out_shape=[
            jax.ShapeDtypeStruct(e.shape, jnp.float32),
            jax.ShapeDtypeStruct(j.shape, jnp.float32),
            jax.ShapeDtypeStruct(dft_e.shape, jnp.float32),
            jax.ShapeDtypeStruct(dft_h.shape, jnp.float32),
            jax.ShapeDtypeStruct((3 * freqs, planes * rx, 2 * cy), jnp.bfloat16),
        ],
        scratch_shapes=[pltpu.VMEM((8, cy), jnp.float32)],
        compiler_params=pltpu.CompilerParams(vmem_limit_bytes=VMEM_ALL),
        cost_estimate=pl.CostEstimate(flops=10 * dft_e.size, bytes_accessed=14 << 20, transcendentals=0),
    )(h, e, j, material, table, rows, cols, dft_e, dft_h)


def signal(sem, where):
    pl.semaphore_signal(sem, inc=1, device_id=where, device_id_type=MESH)


def remote(src, dst, send_sem, recv_sem, where):
    return pltpu.make_async_remote_copy(
        src_ref=src, dst_ref=dst, send_sem=send_sem, recv_sem=recv_sem,
        device_id=where, device_id_type=MESH,
    )


def area_kernel(
    h_any, area_any, patch_ref, skin_ref, counts_ref,
    out_ref, live_ref, rows_ref, cols_ref,
    h_s, area_s, split_s, row_edge, col_edge, counts_s, limit_s, load_sem, send_sem, recv_sem,
):
    comps, pu, pv = area_s.shape
    blocks, cap = patch_ref.shape
    _, planes, rx, cy = h_s.shape
    axes = ("gy", "gx")
    place = [lax.axis_index(axis) for axis in axes]
    count = [lax.axis_size(axis) for axis in axes]
    h_load = pltpu.make_async_copy(h_any, h_s, load_sem.at[0])
    area_load = pltpu.make_async_copy(area_any, area_s, load_sem.at[1])
    h_load.start()
    area_load.start()
    barrier = pltpu.get_barrier_semaphore()
    for axis, at in zip(axes, place):

        @pl.when(at > 0)
        def _():
            signal(barrier, {axis: at - 1})

    h_load.wait()
    col_edge[...] = jnp.zeros_like(col_edge)
    for k in range(2):
        for z in range(planes):
            line = k * planes + z
            row_edge[line : line + 1, :] = h_s[1 + k, z, rx - 1 : rx, :]
            col_edge[line : line + 1, 0:rx] = h_s[2 * k, z].T[cy - 1 : cy, :]
    edges = (row_edge, col_edge)
    landing = (rows_ref, cols_ref)
    copies = [
        remote(edges[i], landing[i], send_sem.at[i], recv_sem.at[i], {axes[i]: place[i] + 1})
        for i in range(2)
    ]
    peers = sum(jnp.where(at < size - 1, 1, 0) for at, size in zip(place, count))

    @pl.when(peers > 0)
    def _():
        pl.semaphore_wait(barrier, peers)

    for i in range(2):

        @pl.when(place[i] < count[i] - 1)
        def _():
            copies[i].start()

        @pl.when(place[i] == 0)
        def _():
            landing[i][...] = jnp.zeros_like(landing[i])

    area_load.wait()
    for c in range(comps):
        high, low = split_two(area_s[c])
        split_s[c, :, 0:pv] = high
        split_s[c, :, pv : 2 * pv] = low
    slots = lax.broadcasted_iota(jnp.int32, (1, cap), 1).astype(jnp.float32)
    counts_s[...] = jnp.zeros_like(counts_s)
    counts_s[0:1, 0:blocks] = counts_ref[...].astype(jnp.float32)
    limit_s[...] = jnp.broadcast_to(counts_s[0:1, :], limit_s.shape[::-1]).T

    def one_group(t, carry):
        for q in range(4):
            first = 8 * t + 2 * q
            ids = jnp.concatenate([patch_ref[pl.ds(first + i, 1), :] for i in range(2)], 1)
            low = (iota0(pv, 2 * cap) == (ids & (pv - 1))).astype(jnp.float32)
            low = low.astype(jnp.bfloat16)
            both = jnp.concatenate([low, low], 0)
            hit = iota0(pu, 2 * cap) == (ids >> shift_of(pv))
            for c in range(comps):
                rows = jnp.dot(split_s[c], both, preferred_element_type=jnp.float32)
                value = jnp.sum(jnp.where(hit, rows, 0.0), axis=0, keepdims=True)
                for i in range(2):
                    out_ref[c, pl.ds(first + i, 1), :] = value[:, i * cap : (i + 1) * cap]
        here = pl.ds(pl.multiple_of(8 * t, 8), 8)
        live_ref[here, :] = jnp.where(slots < limit_s[here, :], skin_ref[here, :], -1)
        return carry

    lax.fori_loop(0, blocks // 8, one_group, 0)
    for i in range(2):

        @pl.when(place[i] < count[i] - 1)
        def _():
            copies[i].wait_send()

        @pl.when(place[i] > 0)
        def _():
            copies[i].wait_recv()


def gather_area(h, area, patch, skin, counts):
    vmem = pl.BlockSpec(memory_space=pltpu.VMEM)
    blocks, cap = patch.shape
    _, planes, rx, cy = h.shape
    edge = (2 * planes, cy)
    lanes = -(-blocks // 128) * 128
    return pl.pallas_call(
        area_kernel,
        in_specs=[pl.BlockSpec(memory_space=pl.ANY)] * 2 + [vmem] * 3,
        out_specs=[vmem] * 4,
        out_shape=[
            jax.ShapeDtypeStruct((area.shape[0],) + patch.shape, jnp.float32),
            jax.ShapeDtypeStruct(skin.shape, jnp.int32),
            jax.ShapeDtypeStruct(edge, jnp.float32),
            jax.ShapeDtypeStruct(edge, jnp.float32),
        ],
        scratch_shapes=[
            pltpu.VMEM(h.shape, jnp.float32),
            pltpu.VMEM(area.shape, jnp.float32),
            pltpu.VMEM((area.shape[0], area.shape[1], 2 * area.shape[2]), jnp.bfloat16),
            pltpu.VMEM(edge, jnp.float32),
            pltpu.VMEM(edge, jnp.float32),
            pltpu.VMEM((8, lanes), jnp.float32),
            pltpu.VMEM((lanes, cap), jnp.float32),
            pltpu.SemaphoreType.DMA((2,)),
            pltpu.SemaphoreType.DMA((2,)),
            pltpu.SemaphoreType.DMA((2,)),
        ],
        compiler_params=pltpu.CompilerParams(
            vmem_limit_bytes=VMEM_ALL, collective_id=0, has_side_effects=True
        ),
    )(h, area, patch, skin, counts)


def flux_pair(flux_ref, live_ref, t):
    rows, hi_count, two_lo = flux_ref.shape
    lo_count = two_lo // 2
    ids = jnp.concatenate([live_ref[pl.ds(2 * t + i, 1), :] for i in range(2)], 1)
    width = ids.shape[1]
    low = (iota0(lo_count, width) == (ids & (lo_count - 1))).astype(jnp.float32)
    low = low.astype(jnp.bfloat16)
    both = jnp.concatenate([low, low], 0)
    hit = iota0(hi_count, width) == (ids >> shift_of(lo_count))
    picked = []
    for r in range(rows):
        part = jnp.dot(flux_ref[r], both, preferred_element_type=jnp.float32)
        picked.append(jnp.sum(jnp.where(hit, part, 0.0), axis=0, keepdims=True))
    return picked


def flux_kernel(flux_ref, live_ref, out_ref, pack_s, send_sem, recv_sem):
    blocks, cap = live_ref.shape
    n_gx = lax.axis_size("gx")
    me = lax.axis_index("gy") * n_gx + lax.axis_index("gx")
    groups = blocks // 8
    barrier = pltpu.get_barrier_semaphore()
    coords = lambda d: (d // n_gx, d % n_gx)
    for k in range(1, blocks):
        signal(barrier, coords((me + k) % blocks))

    def gather_group(group):
        for q in range(4):
            picked = flux_pair(flux_ref, live_ref, group * 4 + q)
            for r, value in enumerate(picked):
                for i in range(2):
                    pack_s[group * 8 + 2 * q + i, r : r + 1, :] = value[:, i * cap : (i + 1) * cap]

    def copy_to(d):
        return remote(pack_s.at[d], out_ref.at[me], send_sem.at[d], recv_sem.at[me], coords(d))

    mine = me // 8
    gather_group(mine)
    out_ref[me] = pack_s[me]
    pl.semaphore_wait(barrier, blocks - 1)
    for k in range(1, 8):
        copy_to(mine * 8 + (me + k) % 8).start()
    gather_group((mine + 1) % groups)

    def one_step(step, carry):
        ready = (mine + step - 1) % groups
        for i in range(8):
            copy_to(ready * 8 + i).start()
        gather_group((mine + step) % groups)
        return carry

    lax.fori_loop(2, groups, one_step, 0)
    last = (mine + groups - 1) % groups
    for i in range(8):
        copy_to(last * 8 + i).start()
    for k in range(1, blocks):
        d = (me + k) % blocks
        copy_to(d).wait_send()
        remote(pack_s.at[d], out_ref.at[d], send_sem.at[d], recv_sem.at[d], coords(d)).wait_recv()


def exchange_flux(flux, live):
    vmem = pl.BlockSpec(memory_space=pltpu.VMEM)
    blocks, cap = live.shape
    shape = (blocks, flux.shape[0], cap)
    return pl.pallas_call(
        flux_kernel,
        in_specs=[vmem, vmem],
        out_specs=vmem,
        out_shape=jax.ShapeDtypeStruct(shape, jnp.float32),
        scratch_shapes=[
            pltpu.VMEM(shape, jnp.float32),
            pltpu.SemaphoreType.DMA((blocks,)),
            pltpu.SemaphoreType.DMA((blocks,)),
        ],
        compiler_params=pltpu.CompilerParams(
            vmem_limit_bytes=40 << 20, collective_id=1, has_side_effects=True
        ),
    )(flux, live)


NT = (((1,), (1,)), ((), ()))
REACH = 104
PAD = 128


def band_kernel(
    rows_ref, area_ref, patch_ref, point_ref, avg_ref,
    dens_s, side_dens, side_patch, hi_own, hi_side, strip_s,
    send_sem, recv_sem, u_send, u_recv,
):
    freqs, pu, pv = point_ref.shape
    blocks, cap = patch_ref.shape
    gy, gx = lax.axis_index("gy"), lax.axis_index("gx")
    n_gy, n_gx = lax.axis_size("gy"), lax.axis_size("gx")
    sides = [("gx", gx > 0, gx - 1), ("gx", gx < n_gx - 1, gx + 1)]
    ends = [("gy", gy > 0, gy - 1), ("gy", gy < n_gy - 1, gy + 1)]
    barrier = pltpu.get_barrier_semaphore()
    for axis, there, at in sides + ends:

        @pl.when(there)
        def _():
            signal(barrier, {axis: at})

    for f in range(freqs):
        dens = area_ref[0] * rows_ref[:, 3 * f, :]
        dens = dens + area_ref[1] * rows_ref[:, 3 * f + 1, :]
        dens_s[f] = dens + area_ref[2] * rows_ref[:, 3 * f + 2, :]
    pl.semaphore_wait(barrier, sum(jnp.where(there, 1, 0) for _, there, _ in sides + ends))
    side_copies = []
    for i, (axis, there, at) in enumerate(sides):
        copies = [
            remote(dens_s, side_dens.at[1 - i], send_sem.at[i, 0], recv_sem.at[1 - i, 0], {axis: at}),
            remote(patch_ref, side_patch.at[1 - i], send_sem.at[i, 1], recv_sem.at[1 - i, 1], {axis: at}),
        ]
        arrivals = [
            remote(dens_s, side_dens.at[i], send_sem.at[i, 0], recv_sem.at[i, 0], {axis: at}),
            remote(patch_ref, side_patch.at[i], send_sem.at[i, 1], recv_sem.at[i, 1], {axis: at}),
        ]
        side_copies.append((there, copies, arrivals))

        @pl.when(there)
        def _():
            for copy in copies:
                copy.start()

        @pl.when(jnp.logical_not(there))
        def _():
            side_dens[i] = jnp.zeros_like(side_dens.at[i])
            side_patch[i] = jnp.zeros_like(side_patch.at[i])

    strip_s[:, 0 : PAD - REACH, :] = jnp.zeros((freqs, PAD - REACH, pv), jnp.float32)
    strip_s[:, pu + PAD + REACH :, :] = jnp.zeros((freqs, PAD - REACH, pv), jnp.float32)
    landing = [pl.ds(PAD - REACH, REACH), pl.ds(PAD + pu, REACH)]
    leaving = [pl.ds(PAD, REACH), pl.ds(PAD + pu - REACH, REACH)]
    for i, (axis, there, at) in enumerate(ends):

        @pl.when(jnp.logical_not(there))
        def _():
            strip_s[:, landing[i], :] = jnp.zeros((freqs, REACH, pv), jnp.float32)

    group = 32 if blocks % 32 == 0 else blocks
    groups = blocks // group

    def rows_of(ids, i):
        return ids[i : i + 1]

    def hi_part(ids, size):
        pieces = [
            (iota0(size, cap) == (rows_of(ids, i) >> shift_of(pv))).astype(jnp.float32)
            for i in range(group)
        ]
        return jnp.concatenate(pieces, 1).astype(jnp.bfloat16)

    def own_step(f, t):
        here = pl.ds(pl.multiple_of(t * group, 8), group)
        ids = patch_ref[here, :]
        if f == 0:
            hi = hi_part(ids, pu)
            hi_own[t] = hi
        else:
            hi = hi_own[t]
        dens = dens_s[f, here, :]
        first = dens.astype(jnp.bfloat16).astype(jnp.float32)
        out = None
        hits = [iota0(pv, cap) == (rows_of(ids, i) & (pv - 1)) for i in range(group)]
        for part in (first, dens - first):
            spread = jnp.concatenate(
                [
                    jnp.where(hits[i], rows_of(part, i), 0.0).astype(jnp.bfloat16)
                    for i in range(group)
                ],
                1,
            )
            one = lax.dot_general(hi, spread, NT, preferred_element_type=jnp.float32)
            out = one if out is None else out + one
        return out

    def own(f):
        point_ref[f] = own_step(f, 0)

        def more(t, carry):
            point_ref[f] += own_step(f, t)
            return carry

        if groups > 1:
            lax.fori_loop(1, groups, more, 0)

    half = pv // 2

    def side_step(f, i, t):
        here = pl.ds(pl.multiple_of(t * group, 8), group)
        ids = side_patch[i, here, :]
        if f == 0:
            hi = hi_part(ids, pu)
            hi_side[i, t] = hi
        else:
            hi = hi_side[i, t]
        dens = side_dens[i, f, here, :]
        first = dens.astype(jnp.bfloat16).astype(jnp.float32)
        rest = dens - first
        pieces = []
        for s in range(group):
            cell = rows_of(ids, s) & (pv - 1)
            if i == 0:
                within = cell >= iota0(half, cap) + (pv - HALF)
            else:
                within = cell <= iota0(half, cap) + (half - 1 - pv + HALF)
            pieces.append(
                jnp.concatenate(
                    [jnp.where(within, rows_of(part, s), 0.0) for part in (first, rest)], 0
                ).astype(jnp.bfloat16)
            )
        out = lax.dot_general(
            hi, jnp.concatenate(pieces, 1), NT, preferred_element_type=jnp.float32
        )
        return out[:, :half] + out[:, half:]

    rows_at = pl.ds(PAD, pu)

    def strip(f):
        k, v = iota0(pv, pv), lax.broadcasted_iota(jnp.int32, (pv, pv), 1)
        band = ((k >= v - HALF) & (k < v + HALF)).astype(jnp.float32).astype(jnp.bfloat16)
        high, low = split_two(point_ref[f])
        mid = jnp.dot(high, band, preferred_element_type=jnp.float32)
        mid = mid + jnp.dot(low, band, preferred_element_type=jnp.float32)
        strip_s[f, rows_at, 0:half] = mid[:, :half] + side_step(f, 0, 0)
        strip_s[f, rows_at, half:pv] = mid[:, half:] + side_step(f, 1, 0)

        def more(t, carry):
            strip_s[f, rows_at, 0:half] += side_step(f, 0, t)
            strip_s[f, rows_at, half:pv] += side_step(f, 1, t)
            return carry

        if groups > 1:
            lax.fori_loop(1, groups, more, 0)

    def end_copy(f, i, arrival):
        axis, there, at = ends[i]
        lands = i if arrival else 1 - i
        return remote(
            strip_s.at[f, leaving[i]], strip_s.at[f, landing[lands]],
            u_send.at[f, i], u_recv.at[f, lands], {axis: at},
        )

    def send_ends(f):
        for i, (axis, there, at) in enumerate(ends):

            @pl.when(there)
            def _():
                end_copy(f, i, False).start()

    def average(f):
        for i, (axis, there, at) in enumerate(ends):

            @pl.when(there)
            def _():
                end_copy(f, i, True).wait_recv()

        u = iota0(pu, pu + 2 * PAD)
        g = lax.broadcasted_iota(jnp.int32, (pu, pu + 2 * PAD), 1) - PAD
        band = ((g >= u - HALF) & (g < u + HALF)).astype(jnp.float32).astype(jnp.bfloat16)
        high, low = split_two(strip_s[f])
        total = jnp.dot(band, high, preferred_element_type=jnp.float32)
        total = total + jnp.dot(band, low, preferred_element_type=jnp.float32)
        avg_ref[f] = total * (1.0 / (4.0 * HALF * HALF))

    own(0)
    own(1)
    for there, copies, arrivals in side_copies:

        @pl.when(there)
        def _():
            for copy in arrivals:
                copy.wait_recv()

    strip(0)
    send_ends(0)
    own(2)
    strip(1)
    send_ends(1)
    strip(2)
    send_ends(2)
    for f in range(freqs):
        average(f)
    for there, copies, arrivals in side_copies:

        @pl.when(there)
        def _():
            for copy in copies:
                copy.wait_send()

    for f in range(freqs):
        for i, (axis, there, at) in enumerate(ends):

            @pl.when(there)
            def _():
                end_copy(f, i, False).wait_send()


def surface(rows, area_rows, patch, pu, pv):
    vmem = pl.BlockSpec(memory_space=pltpu.VMEM)
    blocks, cap = patch.shape
    freqs = rows.shape[1] // 3
    group = 32 if blocks % 32 == 0 else blocks
    out = jax.ShapeDtypeStruct((freqs, pu, pv), jnp.float32)
    return pl.pallas_call(
        band_kernel,
        in_specs=[vmem] * 3,
        out_specs=[vmem] * 2,
        out_shape=[out, out],
        scratch_shapes=[
            pltpu.VMEM((freqs, blocks, cap), jnp.float32),
            pltpu.VMEM((2, freqs, blocks, cap), jnp.float32),
            pltpu.VMEM((2, blocks, cap), jnp.int32),
            pltpu.VMEM((blocks // group, pu, group * cap), jnp.bfloat16),
            pltpu.VMEM((2, blocks // group, pu, group * cap), jnp.bfloat16),
            pltpu.VMEM((freqs, pu + 2 * PAD, pv), jnp.float32),
            pltpu.SemaphoreType.DMA((2, 2)),
            pltpu.SemaphoreType.DMA((2, 2)),
            pltpu.SemaphoreType.DMA((freqs, 2)),
            pltpu.SemaphoreType.DMA((freqs, 2)),
        ],
        compiler_params=pltpu.CompilerParams(
            vmem_limit_bytes=52 << 20, collective_id=2, has_side_effects=True
        ),
    )(rows, area_rows, patch)


def shards(
    e_field, h_field, j_field, material, material_table, dft_e, dft_h, skin_cell, counts,
    patch_slot, area,
):
    blocks, cap = skin_cell.shape[1:]
    patch = patch_slot.reshape(blocks, cap)
    area_rows, live, rows_below, cols_left = gather_area(
        h_field, area, patch, skin_cell.reshape(blocks, cap), counts
    )
    e_next, j_next, dft_e_next, dft_h_next, flux = update_fields(
        h_field, e_field, j_field, material, material_table, rows_below, cols_left, dft_e, dft_h
    )
    arrived = exchange_flux(flux, live)
    point_density, avg_density = surface(arrived, area_rows, patch, area.shape[1], area.shape[2])
    return (e_next, j_next, dft_e_next, dft_h_next, point_density, avg_density)


def solution(mesh):
    placed = (
        P(None, None, "gy", "gx"),
        P(None, None, "gy", "gx"),
        P(None, None, "gy", "gx"),
        P(None, "gy", "gx"),
        P(),
        P(None, None, None, None, "gy", "gx"),
        P(None, None, None, None, "gy", "gx"),
        P(("gy", "gx"), None, None),
        P(("gy", "gx"), None),
        P(("gy", "gx"), None, None),
        P(None, "gy", "gx"),
    )
    return jax.shard_map(
        shards,
        mesh=mesh,
        in_specs=placed,
        out_specs=(
            P(None, None, "gy", "gx"),
            P(None, None, "gy", "gx"),
            P(None, None, None, None, "gy", "gx"),
            P(None, None, None, None, "gy", "gx"),
            P(None, "gy", "gx"),
            P(None, "gy", "gx"),
        ),
        check_vma=False,
    )
```
